512 devices in a mesh: dp: 16 (over y_lo, x, core), tensor: 32 (over y_hi, z).
Axes of the slice: x: 4, y: 8 (y_hi: 4, y_lo: 2; y = y_hi * 2 + y_lo), z: 8, core: 2. Of those that a mesh axis runs over, the one named last changes fastest.
Arguments:
- tokens: bfloat16 [1024, 6144], P('tensor', 'dp'), may hold values from -6 to 6
- in_weight: bfloat16 [6144, 24576], P('dp', 'tensor'), may hold values from -0.078125 to 0.078125
- out_weight: bfloat16 [24576, 6144], P('tensor', 'dp'), may hold values from -0.0390625 to 0.0390625
Outputs:
- teacher: bfloat16 [1024, 6144], P('tensor', 'dp')
- grad_in: float32 [6144, 24576], P('dp', 'tensor')
- grad_out: float32 [24576, 6144], P('tensor', 'dp')
The draws below stay inside these ranges and needn't reach their ends.
All inputs are finite; a program needn't handle non-finite values.
Results may differ from the reference program's by a relative error of at most 0.038.
Values may be sent and summed in bfloat16 or wider, within the bound.
A program may use at most 64 MiB of HBM per device.

```python
import jax
import jax.numpy as jnp
from jax import lax

D = 6144
FF = 24576
TOKENS = 1024
N_DP = 16


def steps_of(own_key, extent, shards, smallest, largest):
    factor_of = 1.0
    for axis_at, blocks in shards:
        steps = jax.random.uniform(jax.random.fold_in(jax.random.fold_in(own_key, 6), axis_at), (blocks,), jnp.float32, smallest / len(shards), largest / len(shards))
        factor_of = factor_of * jnp.repeat(jnp.exp(steps), extent[axis_at] // blocks).reshape((-1,) + (1,) * (len(extent) - 1 - axis_at))
    return factor_of


def bell_draw(rng, dims, deviation, most, shards=(), held_as=jnp.bfloat16):
    drawn = jax.random.normal(rng, dims, jnp.float32) * deviation
    if len(shards) > 0:
        drawn = steps_of(rng, dims, shards, -0.22, 0.18) * drawn
    return jnp.clip(drawn, min=-most, max=most).astype(held_as)


def setup_inputs(seed: int = 0) -> dict:
    keys = jax.random.split(jax.random.key(seed), 4)
    return {
        "tokens": bell_draw(keys[0], (TOKENS, D), 1.0, 6.0, ((0, 32), (1, 16))),
        "in_weight": bell_draw(keys[1], (D, FF), D ** -0.5, 0.078125, ((0, 16), (1, 32))),
        "out_weight": bell_draw(keys[2], (FF, D), FF ** -0.5, 0.0390625, ((0, 32), (1, 16))),
    }


inv_root_two = 0.7071067811865476
inv_root_tau = 0.3989422804014327

def smooth_gate(values):
    return 0.5 * values * (1.0 + lax.erf(values * inv_root_two))

def gate_slope(values):
    return 0.5 * (1.0 + lax.erf(values * inv_root_two)) + values * jnp.exp(-0.5 * values * values) * inv_root_tau

def blocked_sum(left_blocks, right_blocks, width):

    def add_block(running, operands):
        term = jnp.dot(operands[0], operands[1], preferred_element_type=jnp.float32).astype(jnp.bfloat16)
        term = lax.optimization_barrier(term)
        return (running + term.astype(jnp.float32), None)
    start_value = jnp.zeros((left_blocks.shape[1], width), jnp.float32)
    result, _ = lax.scan(add_block, start_value, (left_blocks, right_blocks))
    return result

def reference(tokens, in_weight, out_weight):
    block_width = D // N_DP
    token_blocks = tokens.reshape(TOKENS, N_DP, block_width).transpose(1, 0, 2)
    weight_blocks = in_weight.reshape(N_DP, block_width, FF)
    preact = blocked_sum(token_blocks, weight_blocks, FF).astype(jnp.bfloat16)
    pre_wide = preact.astype(jnp.float32)
    hidden = smooth_gate(pre_wide).astype(jnp.bfloat16)
    first_cut, second_cut, third_cut = (FF // 8, FF // 4, FF // 2)
    student_one = jnp.dot(hidden[:, :first_cut], out_weight[:first_cut], preferred_element_type=jnp.float32)
    student_two = student_one + jnp.dot(hidden[:, first_cut:second_cut], out_weight[first_cut:second_cut], preferred_element_type=jnp.float32)
    student_three = student_two + jnp.dot(hidden[:, second_cut:third_cut], out_weight[second_cut:third_cut], preferred_element_type=jnp.float32)
    full = student_three + jnp.dot(hidden[:, third_cut:], out_weight[third_cut:], preferred_element_type=jnp.float32)
    factor = 1.0 / jnp.sqrt(jnp.float32(TOKENS))
    diff_one = (student_one - full) * factor
    diff_two = (student_two - full) * factor
    diff_three = (student_three - full) * factor
    cot_one = (diff_one + diff_two + diff_three).astype(jnp.bfloat16)
    cot_two = (diff_two + diff_three).astype(jnp.bfloat16)
    cot_three = diff_three.astype(jnp.bfloat16)
    regions = ((0, first_cut, cot_one), (first_cut, second_cut, cot_two), (second_cut, third_cut, cot_three))
    grad_pieces = []
    dhidden_pieces = []
    for low_unit, high_unit, cotangent in regions:
        grad_pieces.append(jnp.dot(hidden[:, low_unit:high_unit].T, cotangent, preferred_element_type=jnp.float32))
        cot_blocks = cotangent.reshape(TOKENS, N_DP, block_width).transpose(1, 0, 2)
        down_blocks = out_weight[low_unit:high_unit].reshape(high_unit - low_unit, N_DP, block_width).transpose(1, 2, 0)
        dhidden_pieces.append(blocked_sum(cot_blocks, down_blocks, high_unit - low_unit))
    grad_pieces.append(jnp.zeros((FF - third_cut, D), jnp.float32))
    dhidden_pieces.append(jnp.zeros((TOKENS, FF - third_cut), jnp.float32))
    grad_out = jnp.concatenate(grad_pieces, axis=0)
    dhidden = jnp.concatenate(dhidden_pieces, axis=1)
    dpre = (dhidden * gate_slope(pre_wide)).astype(jnp.bfloat16)
    grad_in = jnp.dot(tokens.T, dpre, preferred_element_type=jnp.float32)
    return (full.astype(jnp.bfloat16), grad_in, grad_out)
```

```python
import functools

import jax
import jax.numpy as jnp
from jax import lax
from jax.experimental import pallas as pl
from jax.experimental.pallas import tpu as pltpu
from jax.sharding import PartitionSpec as P

inv_root_two = 0.7071067811865476
inv_root_tau = 0.3989422804014327
MESH = pl.DeviceIdType.MESH
BF16 = jnp.bfloat16
F32 = jnp.float32


def smooth_gate(values):
    return 0.5 * values * (1.0 + lax.erf(values * inv_root_two))


def gate_slope(values):
    return (
        0.5 * (1.0 + lax.erf(values * inv_root_two))
        + values * jnp.exp(-0.5 * values * values) * inv_root_tau
    )


def rows(start, size):
    return pl.ds(pl.multiple_of(start, size), size)


def kernel(
    tok_ref, win_hbm, wout_hbm,
    teacher_ref, gin_ref, gout_ref,
    win, wout, tok_all, slope,
    keep, give, sib_in, summed, rs_in,
    hid, contrib, pieces, cots, cot_all,
    keep2, give2, sib_in2, summed2, rs_in2, dpre,
    wsem, ta_s, ta_r, a2_s, a2_r, ct_s, ct_r,
    sb_s, sb_r, rs_s, rs_r, ag_s, ag_r, rl_s, rl_r,
    sb2_s, sb2_r, rs2_s, rs2_r, ag2_s, ag2_r, rl2_s, rl2_r,
):
    d = lax.axis_index("dp")
    t = lax.axis_index("tensor")
    chip = d // 2
    core = d % 2
    other = 1 - core
    sib = chip * 2 + other
    y_hi = t // 8
    z = t % 8

    def remote(src, dst, s_sem, r_sem, dev):
        return pltpu.make_async_remote_copy(
            src_ref=src, dst_ref=dst, send_sem=s_sem, recv_sem=r_sem,
            device_id=dev, device_id_type=MESH,
        )

    w1 = pltpu.make_async_copy(win_hbm, win, wsem.at[0])
    w2 = pltpu.make_async_copy(wout_hbm, wout, wsem.at[1])
    w1.start()
    w2.start()

    barrier = pltpu.get_barrier_semaphore()

    @pl.loop(1, 32)
    def _(i):
        pl.semaphore_signal(barrier, inc=1, device_id={"tensor": (t + i) % 32}, device_id_type=MESH)

    @pl.loop(1, 8)
    def _(i):
        pl.semaphore_signal(
            barrier, inc=1, device_id={"dp": ((chip + i) % 8) * 2 + core}, device_id_type=MESH
        )

    pl.semaphore_signal(barrier, inc=1, device_id={"dp": sib}, device_id_type=MESH)
    tok_all[rows(t * 32, 32), :] = tok_ref[...]
    pl.semaphore_wait(barrier, 39)

    def tok_copy(dst, src_t):
        return remote(
            tok_ref, tok_all.at[rows(src_t * 32, 32)], ta_s.at[dst], ta_r.at[src_t], {"tensor": dst}
        )

    @pl.loop(1, 32)
    def _(i):
        dst = ((y_hi + i % 4) % 4) * 8 + (z + i // 4) % 8
        tok_copy(dst, t).start()

    w1.wait()
    w2.wait()

    def reduce_scatter(ready, block, keep, give, sib_in, summed, rs_in, sb_s, sb_r, rs_s, rs_r):
        def sib_copy(g):
            return remote(give.at[g], sib_in.at[g], sb_s.at[g], sb_r.at[g], {"dp": sib})

        def out_copy(g, src):
            return remote(
                summed.at[g], rs_in.at[src], rs_s.at[g], rs_r.at[src], {"dp": g * 2 + core}
            )

        @pl.loop(0, 9)
        def _(i):
            @pl.when(i < 8)
            def _():
                g = (chip + 1 + i) % 8
                ready(g)
                term = block(g).astype(BF16)
                first, second = term[:64], term[64:]
                mine = core == 0
                keep[g] = jnp.where(mine, first, second)
                give[g] = jnp.where(mine, second, first)
                sib_copy(g).start()

            @pl.when(i > 0)
            def _():
                g = (chip + i) % 8
                sib_copy(g).wait_recv()
                total = (keep[g].astype(F32) + sib_in[g].astype(F32)).astype(BF16)
                summed[g] = total

                @pl.when(g != chip)
                def _():
                    out_copy(g, chip).start()

                @pl.when(g == chip)
                def _():
                    rs_in[g] = total

        @pl.loop(0, 8)
        def _(g):
            sib_copy(g).wait_send()

        @pl.loop(1, 8)
        def _(i):
            out_copy((chip + i) % 8, (chip + 8 - i) % 8).wait()

        total = jnp.zeros((64, 768), F32)
        for g in range(8):
            total = total + rs_in[g].astype(F32)
        return total

    def gather(buf, use, ag_s, ag_r, rl_s, rl_r):
        def out_copy(g, src):
            place = buf.at[rows((src * 2 + core) * 64, 64)]
            return remote(place, place, ag_s.at[g], ag_r.at[src], {"dp": g * 2 + core})

        def relay(src, which):
            place = buf.at[rows((src * 2 + which) * 64, 64)]
            return remote(place, place, rl_s.at[src], rl_r.at[src], {"dp": sib})

        @pl.loop(1, 8)
        def _(i):
            out_copy((chip + i) % 8, chip).start()

        @pl.loop(0, 9)
        def _(i):
            @pl.when(i < 8)
            def _():
                src = (chip + 8 - i) % 8

                @pl.when(i > 0)
                def _():
                    out_copy(chip, src).wait_recv()

                relay(src, core).start()

            @pl.when(i > 0)
            def _():
                src = (chip + 9 - i) % 8
                relay(src, other).wait_recv()
                use(src)

        @pl.loop(0, 8)
        def _(g):
            relay(g, core).wait_send()

        @pl.loop(1, 8)
        def _(i):
            out_copy((chip + i) % 8, chip).wait_send()

    def tok_ready(g):
        @pl.loop(0, 4)
        def _(j):
            src = g * 4 + j

            @pl.when(src != t)
            def _():
                tok_copy(t, src).wait_recv()

    def up(g):
        return jnp.dot(tok_all[rows(g * 128, 128), :], win[...], preferred_element_type=F32)

    pre = reduce_scatter(
        tok_ready, up, keep, give, sib_in, summed, rs_in, sb_s, sb_r, rs_s, rs_r
    )
    pre = pre.astype(BF16).astype(F32)
    slope[...] = gate_slope(pre)
    hid[rows(d * 64, 64), :] = smooth_gate(pre).astype(BF16)

    @pl.loop(1, 32)
    def _(i):
        tok_copy((t + i) % 32, t).wait_send()

    def piece_copy(dst, src_t):
        return remote(
            contrib.at[rows(dst * 32, 32)], pieces.at[src_t], a2_s.at[dst], a2_r.at[src_t],
            {"tensor": dst},
        )

    def down(g):
        contrib[rows(g * 128, 128), :] = jnp.dot(
            hid[rows(g * 128, 128), :], wout[...], preferred_element_type=F32
        ).astype(BF16)

        @pl.loop(0, 4)
        def _(j):
            dst = g * 4 + j

            @pl.when(dst != t)
            def _():
                piece_copy(dst, t).start()

            @pl.when(dst == t)
            def _():
                pieces[t] = contrib[rows(t * 32, 32), :]

    gather(hid, down, ag_s, ag_r, rl_s, rl_r)

    @pl.loop(1, 32)
    def _(i):
        piece_copy((t + i) % 32, (t + 32 - i) % 32).wait()

    def segment(low, high):
        return lax.fori_loop(
            low, high, lambda s, acc: acc + pieces[s].astype(F32), jnp.zeros((32, 384), F32)
        )

    student_one = segment(0, 4)
    student_two = student_one + segment(4, 8)
    student_three = student_two + segment(8, 16)
    full = student_three + segment(16, 32)
    factor = 1.0 / 32.0
    diff_one = (student_one - full) * factor
    diff_two = (student_two - full) * factor
    diff_three = (student_three - full) * factor
    cots[0] = (diff_one + diff_two + diff_three).astype(BF16)
    cots[1] = (diff_two + diff_three).astype(BF16)
    cots[2] = diff_three.astype(BF16)

    def range_of(unit_block):
        return unit_block // 4 - unit_block // 12

    def cot_copy(dst, src_t):
        return remote(
            cots.at[range_of(dst)], cot_all.at[rows(src_t * 32, 32)], ct_s.at[dst], ct_r.at[src_t],
            {"tensor": dst},
        )

    @pl.loop(0, 16)
    def _(i):
        dst = (t + 1 + i) % 16

        @pl.when(dst != t)
        def _():
            cot_copy(dst, t).start()

    teacher_ref[...] = full.astype(BF16)

    @pl.when(t < 16)
    def _():
        cot_all[rows(t * 32, 32), :] = cots[range_of(t)]

        def cot_ready(g):
            @pl.loop(0, 4)
            def _(j):
                src = g * 4 + j

                @pl.when(src != t)
                def _():
                    cot_copy(t, src).wait_recv()

        def back(g):
            return lax.dot_general(
                cot_all[rows(g * 128, 128), :], wout[...], (((1,), (1,)), ((), ())),
                preferred_element_type=F32,
            )

        dhidden = reduce_scatter(
            cot_ready, back, keep2, give2, sib_in2, summed2, rs_in2, sb2_s, sb2_r, rs2_s, rs2_r
        )
        dpre[rows(d * 64, 64), :] = (dhidden * slope[...]).astype(BF16)
        gather(dpre, lambda g: None, ag2_s, ag2_r, rl2_s, rl2_r)
        gin_ref[...] = lax.dot_general(
            tok_all[...], dpre[...], (((0,), (0,)), ((), ())), preferred_element_type=F32
        )
        gout_ref[...] = lax.dot_general(
            hid[...], cot_all[...], (((0,), (0,)), ((), ())), preferred_element_type=F32
        )

    @pl.when(t >= 16)
    def _():
        gin_ref[...] = jnp.zeros_like(gin_ref)
        gout_ref[...] = jnp.zeros_like(gout_ref)

    @pl.loop(0, 16)
    def _(i):
        @pl.when(i != t)
        def _():
            cot_copy(i, t).wait_send()


def shards(tokens, in_weight, out_weight):
    vmem = pl.BlockSpec(memory_space=pltpu.VMEM)
    hbm = pl.BlockSpec(memory_space=pl.ANY)
    dma = pltpu.SemaphoreType.DMA
    block = pltpu.VMEM((8, 64, 768), BF16)
    return pl.pallas_call(
        kernel,
        out_shape=(
            jax.ShapeDtypeStruct((32, 384), BF16),
            jax.ShapeDtypeStruct((384, 768), F32),
            jax.ShapeDtypeStruct((768, 384), F32),
        ),
        in_specs=[vmem, hbm, hbm],
        out_specs=(vmem, vmem, vmem),
        scratch_shapes=[
            pltpu.VMEM((384, 768), BF16),
            pltpu.VMEM((768, 384), BF16),
            pltpu.VMEM((1024, 384), BF16),
            pltpu.VMEM((64, 768), F32),
            block, block, block, block, block,
            pltpu.VMEM((1024, 768), BF16),
            pltpu.VMEM((1024, 384), BF16),
            pltpu.VMEM((32, 32, 384), BF16),
            pltpu.VMEM((3, 32, 384), BF16),
            pltpu.VMEM((1024, 384), BF16),
            block, block, block, block, block,
            pltpu.VMEM((1024, 768), BF16),
            dma((2,)),
        ]
        + [dma((32,))] * 6
        + [dma((8,))] * 16,
        compiler_params=pltpu.CompilerParams(
            collective_id=0, has_side_effects=True, vmem_limit_bytes=48 * 1024 * 1024
        ),
        cost_estimate=pl.CostEstimate(
            flops=5 * 2 * 1024 * 384 * 768, bytes_accessed=4_000_000, transcendentals=100_000
        ),
    )(tokens, in_weight, out_weight)


def solution(mesh):
    in_specs = (P("tensor", "dp"), P("dp", "tensor"), P("tensor", "dp"))
    out_specs = (P("tensor", "dp"), P("dp", "tensor"), P("tensor", "dp"))
    return jax.shard_map(shards, mesh=mesh, in_specs=in_specs, out_specs=out_specs, check_vma=False)
```

```python
import jax
import jax.numpy as jnp
from jax import lax
from jax.experimental import pallas as pl
from jax.experimental.pallas import tpu as pltpu
from jax.sharding import PartitionSpec as P

inv_root_two = 0.7071067811865476
inv_root_tau = 0.3989422804014327
MESH = pl.DeviceIdType.MESH
BF16 = jnp.bfloat16
F32 = jnp.float32
LAG_SUM, LAG_HID, LAG_ALL, LAG_USE = 1, 4, 7, 8


def smooth_gate(values):
    return 0.5 * values * (1.0 + lax.erf(values * inv_root_two))


def gate_slope(values):
    return (
        0.5 * (1.0 + lax.erf(values * inv_root_two))
        + values * jnp.exp(-0.5 * values * values) * inv_root_tau
    )


def rows(start, size, step=None):
    return pl.ds(pl.multiple_of(start, step or size), size)


def kernel(
    tok_hbm, win_hbm, wout_hbm,
    teacher_ref, gin_ref, gout_ref,
    win, wout, tok_all, slope, hid, contrib, z_in, y_out, y_in,
    cots, cot_y, cot_all, dpre,
    keep, give, sib_in, summed, rs_in,
    keep2, give2, sib_in2, summed2, rs_in2,
    wsem, tok_s, tok_r, zin_s, zin_r, yin_s, yin_r, cy_s, cy_r, ct_s, ct_r,
    sb_s, sb_r, rs_s, rs_r, ag_s, ag_r, rl_s, rl_r,
    sb2_s, sb2_r, rs2_s, rs2_r, ag2_s, ag2_r, rl2_s, rl2_r,
):
    d = lax.axis_index("dp")
    t = lax.axis_index("tensor")
    chip = d // 2
    core = d % 2
    sib = chip * 2 + 1 - core
    y = t // 8
    z = t % 8

    def remote(src, dst, s_sem, r_sem, dev):
        return pltpu.make_async_remote_copy(
            src_ref=src, dst_ref=dst, send_sem=s_sem, recv_sem=r_sem,
            device_id=dev, device_id_type=MESH,
        )

    def drain_send(ref, sem):
        remote(ref, ref, sem, sem, {"dp": sib}).wait_send()

    def drain_recv(ref, sem):
        remote(ref, ref, sem, sem, {"dp": sib}).wait_recv()

    def offset(i):
        n = (8 - i) % 8
        return ((n + 1) // 2) * (2 * (n % 2) - 1)

    def along_z(i):
        return (z + offset(i) + 8) % 8

    mine = tok_all.at[rows(y * 32, 32)]
    w0 = pltpu.make_async_copy(tok_hbm, mine, wsem.at[0])
    w1 = pltpu.make_async_copy(win_hbm, win, wsem.at[1])
    w2 = pltpu.make_async_copy(wout_hbm, wout, wsem.at[2])
    w0.start()
    w1.start()
    w2.start()

    barrier = pltpu.get_barrier_semaphore()

    @pl.loop(1, 8)
    def _(i):
        pl.semaphore_signal(
            barrier, inc=1, device_id={"tensor": y * 8 + (z + i) % 8}, device_id_type=MESH
        )
        pl.semaphore_signal(
            barrier, inc=1, device_id={"dp": ((chip + i) % 8) * 2 + core}, device_id_type=MESH
        )

    @pl.loop(1, 4)
    def _(i):
        pl.semaphore_signal(
            barrier, inc=1, device_id={"tensor": ((y + i) % 4) * 8 + z}, device_id_type=MESH
        )

    pl.semaphore_signal(barrier, inc=1, device_id={"dp": sib}, device_id_type=MESH)
    w0.wait()
    pl.semaphore_wait(barrier, 18)

    def chunk_to(i, k, src, all_ref, s_sem, r_sem):
        return remote(
            src, all_ref.at[rows(i * 128 + k * 32, 32)], s_sem, r_sem.at[i],
            {"tensor": y * 8 + along_z(i)},
        )

    @pl.loop(1, 4)
    def _(j):
        k = (y + 1 + j % 3) % 4
        remote(mine, mine, tok_s, tok_r.at[0], {"tensor": k * 8 + z}).start()

    @pl.loop(1, 8)
    def _(i):
        chunk_to(i, y, mine, tok_all, tok_s, tok_r).start()

    drain_recv(tok_all.at[rows(0, 96)], tok_r.at[0])

    @pl.loop(1, 8)
    def _(i):
        @pl.loop(1, 4)
        def _(j):
            k = (y + j) % 4
            chunk_to(i, k, tok_all.at[rows(k * 32, 32)], tok_all, tok_s, tok_r).start()

    w1.wait()
    w2.wait()

    def pipeline(
        ready, block, finish, use, full_buf,
        keep, give, sib_in, summed, rs_in, sb_s, sb_r, rs_s, rs_r, ag_s, ag_r, rl_s, rl_r,
    ):
        def sib_copy(i):
            return remote(give.at[i], sib_in.at[i], sb_s, sb_r.at[i], {"dp": sib})

        def relay(i):
            place = full_buf.at[core, rows(i * 128, 128)]
            return remote(place, place, rl_s, rl_r.at[i], {"dp": sib})

        @pl.loop(0, 8 + LAG_USE)
        def _(s):
            @pl.when(s < 8)
            def _():
                ready(s)
                term = block(s).astype(BF16)
                first, second = term[:, :384], term[:, 384:]
                keep[s] = jnp.where(core == 0, first, second)
                give[s] = jnp.where(core == 0, second, first)
                sib_copy(s).start()

            @pl.when((s >= LAG_SUM) & (s < LAG_SUM + 8))
            def _():
                i = s - LAG_SUM
                sib_copy(i).wait_recv()
                total = (keep[i].astype(F32) + sib_in[i].astype(F32)).astype(BF16)
                summed[rows(i * 128, 128), :] = total

                @pl.loop(1, 8)
                def _(j):
                    c = (chip + j) % 8
                    remote(
                        summed.at[rows(i * 128 + c * 16, 16)],
                        rs_in.at[rows(i * 128 + chip * 16, 16)],
                        rs_s, rs_r.at[i], {"dp": c * 2 + core},
                    ).start()

                own = rows(i * 128 + chip * 16, 16)
                rs_in[own, :] = summed[own, :]

            @pl.when((s >= LAG_HID) & (s < LAG_HID + 8))
            def _():
                i = s - LAG_HID
                drain_recv(rs_in.at[rows(i * 128, 112, 128)], rs_r.at[i])
                total = jnp.zeros((16, 384), F32)
                for c in range(8):
                    total = total + rs_in[rows(i * 128 + c * 16, 16), :].astype(F32)
                own = rows(i * 128 + chip * 16, 16)
                full_buf[core, own, :] = finish(i, total)
                place = full_buf.at[core, own]

                @pl.loop(1, 8)
                def _(j):
                    c = (chip + j) % 8
                    remote(place, place, ag_s, ag_r.at[i], {"dp": c * 2 + core}).start()

            @pl.when((s >= LAG_ALL) & (s < LAG_ALL + 8))
            def _():
                i = s - LAG_ALL
                drain_recv(full_buf.at[core, rows(i * 128, 112, 128)], ag_r.at[i])
                relay(i).start()

            @pl.when(s >= LAG_USE)
            def _():
                i = s - LAG_USE
                relay(i).wait_recv()
                use(i)

        drain_send(give, sb_s)
        drain_send(summed.at[rows(0, 896)], rs_s)
        drain_send(full_buf.at[0, rows(0, 896)], ag_s)
        drain_send(full_buf.at[0], rl_s)

    def tok_ready(i):
        @pl.when(i > 0)
        def _():
            drain_recv(tok_all.at[rows(i * 128, 128)], tok_r.at[i])

    def up(i):
        return jnp.dot(tok_all[rows(i * 128, 128), :], win[...], preferred_element_type=F32)

    def hidden_of(i, total):
        pre = total.astype(BF16).astype(F32)
        slope[i] = gate_slope(pre)
        return smooth_gate(pre).astype(BF16)

    def down(i):
        group = rows(i * 128, 128)
        out = jnp.dot(hid[0, group, :], wout[:384, :], preferred_element_type=F32)
        out = out + jnp.dot(hid[1, group, :], wout[384:, :], preferred_element_type=F32)

        @pl.when(i == 0)
        def _():
            z_in[z] = out.astype(BF16)

        @pl.when(i > 0)
        def _():
            contrib[i] = out.astype(BF16)
            dst = (z - offset(i) + 8) % 8
            remote(contrib.at[i], z_in.at[z], zin_s, zin_r, {"tensor": y * 8 + dst}).start()

    pipeline(
        tok_ready, up, hidden_of, down, hid,
        keep, give, sib_in, summed, rs_in, sb_s, sb_r, rs_s, rs_r, ag_s, ag_r, rl_s, rl_r,
    )

    drain_recv(z_in.at[pl.ds(0, 7)], zin_r)

    def y_copy(which, k, slot):
        return remote(
            y_out.at[which, k], y_in.at[slot], yin_s.at[which, k], yin_r.at[slot],
            {"tensor": k * 8 + z},
        )

    slot = y + (y + 3) // 4

    @pl.loop(0, 4)
    def _(j):
        k = (y + 2 + j + j // 2 + j // 3 * 2) % 4
        part = rows(k * 32, 32)
        low = jnp.zeros((32, 384), F32)
        high = jnp.zeros((32, 384), F32)
        for s in range(4):
            low = low + z_in[s, part, :].astype(F32)
            high = high + z_in[s + 4, part, :].astype(F32)

        @pl.when(y == 0)
        def _():
            y_out[0, k] = low.astype(BF16)
            y_out[1, k] = high.astype(BF16)

        @pl.when(y > 0)
        def _():
            y_out[0, k] = (low + high).astype(BF16)

        @pl.when(k != y)
        def _():
            y_copy(0, k, slot).start()

            @pl.when(y == 0)
            def _():
                y_copy(1, k, 1).start()

        @pl.when(k == y)
        def _():
            y_in[slot] = y_out[0, k]

            @pl.when(y == 0)
            def _():
                y_in[1] = y_out[1, k]

    @pl.loop(0, 5)
    def _(s):
        @pl.when(s - (s + 4) // 5 != y)
        def _():
            y_copy(0, y, s).wait_recv()

    student_one = y_in[0].astype(F32)
    student_two = student_one + y_in[1].astype(F32)
    student_three = student_two + y_in[2].astype(F32)
    full = student_three + (y_in[3].astype(F32) + y_in[4].astype(F32))
    factor = 1.0 / 32.0
    diff_one = (student_one - full) * factor
    diff_two = (student_two - full) * factor
    diff_three = (student_three - full) * factor
    cots[0] = (diff_one + diff_two + diff_three).astype(BF16)
    cots[1] = (diff_two + diff_three).astype(BF16)
    cots[2] = diff_three.astype(BF16)

    def cot_y_copy(which):
        dst = which // 2
        return remote(
            cots.at[which], cot_y.at[which % 2, rows(y * 32, 32)], cy_s.at[which],
            cy_r.at[which % 2, y], {"tensor": dst * 8 + z},
        )

    for which in range(3):
        @pl.when(y != which // 2)
        def _(which=which):
            cot_y_copy(which).start()

        @pl.when(y == which // 2)
        def _(which=which):
            cot_y[which % 2, rows(y * 32, 32), :] = cots[which]

    teacher_ref[...] = full.astype(BF16)

    @pl.when(y < 2)
    def _():
        def cot_chunk(i, k):
            kind = (1 - y) * (along_z(i) // 4)
            return chunk_to(i, k, cot_y.at[kind, rows(k * 32, 32)], cot_all, ct_s, ct_r)

        @pl.loop(1, 8)
        def _(i):
            cot_chunk(i, y).start()

        @pl.loop(1, 4)
        def _(j):
            k = (y + j) % 4
            part = cot_y.at[0, rows(k * 32, 32)]
            drain_recv(part, cy_r.at[0, k])

            @pl.when(y == 0)
            def _():
                drain_recv(part, cy_r.at[1, k])

        @pl.loop(1, 8)
        def _(i):
            @pl.loop(1, 4)
            def _(j):
                cot_chunk(i, (y + j) % 4).start()

        cot_all[rows(0, 128), :] = cot_y[(1 - y) * (z // 4)]

        def cot_ready(i):
            @pl.when(i > 0)
            def _():
                drain_recv(cot_all.at[rows(i * 128, 128)], ct_r.at[i])

        def back(i):
            return lax.dot_general(
                cot_all[rows(i * 128, 128), :], wout[...], (((1,), (1,)), ((), ())),
                preferred_element_type=F32,
            )

        def dpre_of(i, total):
            return (total * slope[i]).astype(BF16)

        def over_tokens(left, right):
            return lax.dot_general(
                left, right, (((0,), (0,)), ((), ())), preferred_element_type=F32
            )

        def grads(i):
            @pl.when(i == 4)
            def _():
                for h in range(2):
                    gout_ref[h * 384 : h * 384 + 384, :] = over_tokens(hid[h], cot_all[...])

        pipeline(
            cot_ready, back, dpre_of, grads, dpre,
            keep2, give2, sib_in2, summed2, rs_in2,
            sb2_s, sb2_r, rs2_s, rs2_r, ag2_s, ag2_r, rl2_s, rl2_r,
        )
        for h in range(2):
            gin_ref[:, h * 384 : h * 384 + 384] = over_tokens(tok_all[...], dpre[h])
        drain_send(cot_all.at[rows(0, 896)], ct_s)

    @pl.when(y >= 2)
    def _():
        gin_ref[...] = jnp.zeros_like(gin_ref)
        gout_ref[...] = jnp.zeros_like(gout_ref)

    for which in range(3):
        @pl.when(y != which // 2)
        def _(which=which):
            cot_y_copy(which).wait_send()

    @pl.loop(1, 4)
    def _(j):
        k = (y + j) % 4
        y_copy(0, k, 0).wait_send()

        @pl.when(y == 0)
        def _():
            y_copy(1, k, 0).wait_send()

    drain_send(z_in.at[pl.ds(0, 7)], zin_s)
    drain_send(tok_all.at[rows(0, 992)], tok_s)


def shards(tokens, in_weight, out_weight):
    vmem = pl.BlockSpec(memory_space=pltpu.VMEM)
    hbm = pl.BlockSpec(memory_space=pl.ANY)
    dma = pltpu.SemaphoreType.DMA
    one = dma(())
    block = pltpu.VMEM((8, 128, 384), BF16)
    flat = pltpu.VMEM((1024, 384), BF16)
    return pl.pallas_call(
        kernel,
        out_shape=(
            jax.ShapeDtypeStruct((32, 384), BF16),
            jax.ShapeDtypeStruct((384, 768), F32),
            jax.ShapeDtypeStruct((768, 384), F32),
        ),
        in_specs=[hbm, hbm, hbm],
        out_specs=(vmem, vmem, vmem),
        scratch_shapes=[
            pltpu.VMEM((384, 768), BF16),
            pltpu.VMEM((768, 384), BF16),
            flat,
            pltpu.VMEM((8, 16, 384), F32),
            pltpu.VMEM((2, 1024, 384), BF16),
            block,
            block,
            pltpu.VMEM((2, 4, 32, 384), BF16),
            pltpu.VMEM((5, 32, 384), BF16),
            pltpu.VMEM((3, 32, 384), BF16),
            pltpu.VMEM((2, 128, 384), BF16),
            flat,
            pltpu.VMEM((2, 1024, 384), BF16),
        ]
        + [block, block, block, flat, flat] * 2
        + [
            dma((3,)),
            one, dma((8,)),
            one, one,
            dma((2, 4)), dma((5,)),
            dma((3,)), dma((2, 4)),
            one, dma((8,)),
        ]
        + [one, dma((8,))] * 8,
        compiler_params=pltpu.CompilerParams(
            collective_id=0, has_side_effects=True, vmem_limit_bytes=60 * 1024 * 1024
        ),
        cost_estimate=pl.CostEstimate(
            flops=5 * 2 * 1024 * 384 * 768, bytes_accessed=4_000_000, transcendentals=100_000
        ),
    )(tokens, in_weight, out_weight)


def solution(mesh):
    in_specs = (P("tensor", "dp"), P("dp", "tensor"), P("tensor", "dp"))
    out_specs = (P("tensor", "dp"), P("dp", "tensor"), P("tensor", "dp"))
    return jax.shard_map(shards, mesh=mesh, in_specs=in_specs, out_specs=out_specs, check_vma=False)
```

```python
import jax
import jax.numpy as jnp
from jax import lax
from jax.experimental import pallas as pl
from jax.experimental.pallas import tpu as pltpu
from jax.sharding import PartitionSpec as P

inv_root_two = 0.7071067811865476
inv_root_tau = 0.3989422804014327
MESH = pl.DeviceIdType.MESH
BF16 = jnp.bfloat16
F32 = jnp.float32
FORWARD_LAGS = (1, 4, 7, 9)
BACKWARD_LAGS = (1, 6, 11, 13)
FAR = 3


def smooth_gate(values):
    return 0.5 * values * (1.0 + lax.erf(values * inv_root_two))


def gate_slope(values):
    return (
        0.5 * (1.0 + lax.erf(values * inv_root_two))
        + values * jnp.exp(-0.5 * values * values) * inv_root_tau
    )


def over_tokens(left, right):
    return lax.dot_general(
        left, right, (((0,), (0,)), ((), ())), preferred_element_type=F32
    )


def rows(start, size, step=None):
    return pl.ds(pl.multiple_of(start, step or size), size)


def kernel(
    tok_hbm, win_hbm, wout_hbm,
    teacher_ref, tok_all, dpre, gout_ref,
    win, wout, slope, hid, contrib, z_in, y_out, y_in,
    cots, cot_y, cot_far, cot_all,
    keep, give, sib_in, summed, rs_in,
    keep2, give2, sib_in2, summed2, rs_in2,
    wsem, tok_s, tok_r, far_r, zin_s, zin_r, yin_s, yin_r, cy_s, cy_r, ct_s, ct_r,
    cfar_s, cfar_r, cfw_s, cfw_r,
    sb_s, sb_r, rs_s, rs_r, ag_s, ag_r, rl_s, rl_r,
    sb2_s, sb2_r, rs2_s, rs2_r, ag2_s, ag2_r, rl2_s, rl2_r,
):
    d = lax.axis_index("dp")
    t = lax.axis_index("tensor")
    chip = d // 2
    core = d % 2
    sib = chip * 2 + 1 - core
    y = t // 8
    z = t % 8

    def remote(src, dst, s_sem, r_sem, dev):
        return pltpu.make_async_remote_copy(
            src_ref=src, dst_ref=dst, send_sem=s_sem, recv_sem=r_sem,
            device_id=dev, device_id_type=MESH,
        )

    def drain_send(ref, sem):
        remote(ref, ref, sem, sem, {"dp": sib}).wait_send()

    def drain_recv(ref, sem):
        remote(ref, ref, sem, sem, {"dp": sib}).wait_recv()

    def offset(i):
        n = (8 - i) % 8
        return ((n + 1) // 2) * (2 * (n % 2) - 1)

    def along_z(i):
        return (z + offset(i) + 8) % 8

    mine = tok_all.at[rows(y * 32, 32)]
    w0 = pltpu.make_async_copy(tok_hbm, mine, wsem.at[0])
    w1 = pltpu.make_async_copy(win_hbm, win, wsem.at[1])
    w2 = pltpu.make_async_copy(wout_hbm, wout, wsem.at[2])
    w0.start()
    w1.start()
    w2.start()

    barrier = pltpu.get_barrier_semaphore()

    @pl.loop(1, 8)
    def _(i):
        pl.semaphore_signal(
            barrier, inc=1, device_id={"tensor": y * 8 + (z + i) % 8}, device_id_type=MESH
        )
        pl.semaphore_signal(
            barrier, inc=1, device_id={"dp": ((chip + i) % 8) * 2 + core}, device_id_type=MESH
        )

    @pl.loop(1, 4)
    def _(i):
        pl.semaphore_signal(
            barrier, inc=1, device_id={"tensor": ((y + i) % 4) * 8 + z}, device_id_type=MESH
        )

    pl.semaphore_signal(barrier, inc=1, device_id={"dp": sib}, device_id_type=MESH)
    w0.wait()
    pl.semaphore_wait(barrier, 18)

    @pl.loop(1, FAR + 1)
    def _(i):
        remote(
            mine, tok_all.at[rows(i * 128 + y * 32, 32)], tok_s, tok_r.at[i],
            {"tensor": y * 8 + along_z(i)},
        ).start()

    @pl.loop(0, 3)
    def _(j):
        k = (y + 1 + (j + 1) % 3) % 4
        remote(mine, mine, tok_s, tok_r.at[0], {"tensor": k * 8 + z}).start()

    drain_recv(tok_all.at[rows(0, 96)], tok_r.at[0])

    @pl.loop(FAR + 1, 8)
    def _(i):
        remote(
            tok_all.at[rows(0, 128)], tok_all.at[rows(i * 128, 128)], tok_s, tok_r.at[i],
            {"tensor": y * 8 + along_z(i)},
        ).start()

    @pl.loop(1, FAR + 1)
    def _(i):
        part = tok_all.at[rows(i * 128 + y * 32, 32)]
        drain_recv(part, tok_r.at[i])

        @pl.loop(0, 3)
        def _(j):
            k = (y + 1 + (j + 1) % 3) % 4
            remote(part, part, tok_s, far_r.at[i], {"tensor": k * 8 + z}).start()

    w1.wait()
    w2.wait()

    def pipeline(
        lags, ready, block, finish, use, full_buf,
        keep, give, sib_in, summed, rs_in, sb_s, sb_r, rs_s, rs_r, ag_s, ag_r, rl_s, rl_r,
    ):
        def sib_copy(i):
            return remote(give.at[i], sib_in.at[i], sb_s, sb_r.at[i], {"dp": sib})

        def relay(i):
            place = full_buf.at[core, rows(i * 128, 128)]
            return remote(place, place, rl_s, rl_r.at[i], {"dp": sib})

        lag_sum, lag_hid, lag_all, lag_use = lags

        @pl.loop(0, 8 + lag_use)
        def _(s):
            @pl.when(s >= lag_use)
            def _():
                i = s - lag_use
                relay(i).wait_recv()
                use(i)

            @pl.when((s >= lag_all) & (s < lag_all + 8))
            def _():
                i = s - lag_all
                drain_recv(full_buf.at[core, rows(i * 128, 112, 128)], ag_r.at[i])
                relay(i).start()

            @pl.when((s >= lag_hid) & (s < lag_hid + 8))
            def _():
                i = s - lag_hid
                drain_recv(rs_in.at[rows(i * 128, 112, 128)], rs_r.at[i])
                total = jnp.zeros((16, 384), F32)
                for c in range(8):
                    total = total + rs_in[rows(i * 128 + c * 16, 16), :].astype(F32)
                own = rows(i * 128 + chip * 16, 16)
                full_buf[core, own, :] = finish(i, total)
                place = full_buf.at[core, own]

                @pl.loop(1, 8)
                def _(j):
                    c = (chip + j) % 8
                    remote(place, place, ag_s, ag_r.at[i], {"dp": c * 2 + core}).start()

            @pl.when((s >= lag_sum) & (s < lag_sum + 8))
            def _():
                i = s - lag_sum
                sib_copy(i).wait_recv()
                total = (keep[i].astype(F32) + sib_in[i].astype(F32)).astype(BF16)
                summed[rows(i * 128, 128), :] = total

                @pl.loop(1, 8)
                def _(j):
                    c = (chip + j) % 8
                    remote(
                        summed.at[rows(i * 128 + c * 16, 16)],
                        rs_in.at[rows(i * 128 + chip * 16, 16)],
                        rs_s, rs_r.at[i], {"dp": c * 2 + core},
                    ).start()

                own = rows(i * 128 + chip * 16, 16)
                rs_in[own, :] = summed[own, :]

            @pl.when(s < 8)
            def _():
                ready(s)
                term = block(s).astype(BF16)
                first, second = term[:, :384], term[:, 384:]
                keep[s] = jnp.where(core == 0, first, second)
                give[s] = jnp.where(core == 0, second, first)
                sib_copy(s).start()

        drain_send(give, sb_s)
        drain_send(summed.at[rows(0, 896)], rs_s)
        drain_send(full_buf.at[0, rows(0, 896)], ag_s)
        drain_send(full_buf.at[0], rl_s)

    def ready_of(all_ref, near_r, far_r, i):
        @pl.when(i > FAR)
        def _():
            drain_recv(all_ref.at[rows(i * 128, 128)], near_r.at[i])

        @pl.when((i > 0) & (i <= FAR))
        def _():
            drain_recv(all_ref.at[rows(i * 128, 96, 128)], far_r.at[i])

    def tok_ready(i):
        ready_of(tok_all, tok_r, far_r, i)

    def up(i):
        return jnp.dot(tok_all[rows(i * 128, 128), :], win[...], preferred_element_type=F32)

    def hidden_of(i, total):
        pre = total.astype(BF16).astype(F32)
        slope[i] = gate_slope(pre)
        return smooth_gate(pre).astype(BF16)

    def down(i):
        group = rows(i * 128, 128)
        out = jnp.dot(hid[0, group, :], wout[:384, :], preferred_element_type=F32)
        out = out + jnp.dot(hid[1, group, :], wout[384:, :], preferred_element_type=F32)

        @pl.when(i == 0)
        def _():
            z_in[z] = out.astype(BF16)

        @pl.when(i > 0)
        def _():
            contrib[i] = out.astype(BF16)
            dst = (z - offset(i) + 8) % 8
            remote(contrib.at[i], z_in.at[z], zin_s, zin_r, {"tensor": y * 8 + dst}).start()

    pipeline(
        FORWARD_LAGS, tok_ready, up, hidden_of, down, hid,
        keep, give, sib_in, summed, rs_in, sb_s, sb_r, rs_s, rs_r, ag_s, ag_r, rl_s, rl_r,
    )

    drain_recv(z_in.at[pl.ds(0, 7)], zin_r)

    def y_copy(which, k, slot):
        return remote(
            y_out.at[which, k], y_in.at[slot], yin_s.at[which, k], yin_r.at[slot],
            {"tensor": k * 8 + z},
        )

    slot = y + (y + 3) // 4

    @pl.loop(0, 4)
    def _(j):
        k = (y + 2 + j + j // 2 + j // 3 * 2) % 4
        part = rows(k * 32, 32)
        low = jnp.zeros((32, 384), F32)
        high = jnp.zeros((32, 384), F32)
        for s in range(4):
            low = low + z_in[s, part, :].astype(F32)
            high = high + z_in[s + 4, part, :].astype(F32)

        @pl.when(y == 0)
        def _():
            y_out[0, k] = low.astype(BF16)
            y_out[1, k] = high.astype(BF16)

        @pl.when(y > 0)
        def _():
            y_out[0, k] = (low + high).astype(BF16)

        @pl.when(k != y)
        def _():
            y_copy(0, k, slot).start()

            @pl.when(y == 0)
            def _():
                y_copy(1, k, 1).start()

        @pl.when(k == y)
        def _():
            y_in[slot] = y_out[0, k]

            @pl.when(y == 0)
            def _():
                y_in[1] = y_out[1, k]

    @pl.loop(0, 5)
    def _(s):
        @pl.when(s - (s + 4) // 5 != y)
        def _():
            y_copy(0, y, s).wait_recv()

    student_one = y_in[0].astype(F32)
    student_two = student_one + y_in[1].astype(F32)
    student_three = student_two + y_in[2].astype(F32)
    full = student_three + (y_in[3].astype(F32) + y_in[4].astype(F32))
    factor = 1.0 / 32.0
    diff_one = (student_one - full) * factor
    diff_two = (student_two - full) * factor
    diff_three = (student_three - full) * factor
    cots[0] = (diff_one + diff_two + diff_three).astype(BF16)
    cots[1] = (diff_two + diff_three).astype(BF16)
    cots[2] = diff_three.astype(BF16)

    def cot_y_copy(which):
        dst = which // 2
        return remote(
            cots.at[which], cot_y.at[which % 2, rows(y * 32, 32)], cy_s.at[which],
            cy_r.at[which % 2, y], {"tensor": dst * 8 + z},
        )

    for which in range(3):
        @pl.when(y != which // 2)
        def _(which=which):
            cot_y_copy(which).start()

        @pl.when(y == which // 2)
        def _(which=which):
            cot_y[which % 2, rows(y * 32, 32), :] = cots[which]

    @pl.loop(1, FAR + 1)
    def _(i):
        z_to = along_z(i)
        for row in range(2):
            kind = z_to // 4 if row == 0 else 2
            remote(
                cots.at[kind], cot_far.at[i, rows(row * 32, 32)], cfar_s, cfar_r.at[i],
                {"tensor": y * 8 + z_to},
            ).start()

    teacher_ref[...] = full.astype(BF16)

    @pl.when(y < 2)
    def _():
        @pl.loop(1, 4)
        def _(j):
            k = (y + j) % 4
            part = cot_y.at[0, rows(k * 32, 32)]
            drain_recv(part, cy_r.at[0, k])

            @pl.when(y == 0)
            def _():
                drain_recv(part, cy_r.at[1, k])

        @pl.loop(FAR + 1, 8)
        def _(i):
            kind = (1 - y) * (along_z(i) // 4)
            remote(
                cot_y.at[kind], cot_all.at[rows(i * 128, 128)], ct_s, ct_r.at[i],
                {"tensor": y * 8 + along_z(i)},
            ).start()

        cot_all[rows(0, 128), :] = cot_y[(1 - y) * (z // 4)]

    @pl.loop(1, FAR + 1)
    def _(i):
        drain_recv(cot_far.at[i], cfar_r.at[i])
        place = rows(i * 128 + y * 32, 32)
        for row in range(2):
            part = cot_far.at[i, rows(row * 32, 32)]

            @pl.when(y != row)
            def _(part=part, row=row):
                remote(
                    part, cot_all.at[place], cfw_s, cfw_r.at[i], {"tensor": row * 8 + z}
                ).start()

            @pl.when(y == row)
            def _(part=part):
                cot_all[place, :] = part[...]

    @pl.when(y < 2)
    def _():
        def cot_ready(i):
            ready_of(cot_all, ct_r, cfw_r, i)

        def back(i):
            return lax.dot_general(
                cot_all[rows(i * 128, 128), :], wout[...], (((1,), (1,)), ((), ())),
                preferred_element_type=F32,
            )

        def dpre_of(i, total):
            return (total * slope[i]).astype(BF16)

        def grads(i):
            @pl.when(i == 4)
            def _():
                for h in range(2):
                    gout_ref[h * 384 : h * 384 + 384, :] = over_tokens(hid[h], cot_all[...])

        pipeline(
            BACKWARD_LAGS, cot_ready, back, dpre_of, grads, dpre,
            keep2, give2, sib_in2, summed2, rs_in2,
            sb2_s, sb2_r, rs2_s, rs2_r, ag2_s, ag2_r, rl2_s, rl2_r,
        )
        drain_send(cot_all.at[rows(0, 128 * (7 - FAR))], ct_s)
        drain_send(cot_all.at[rows(0, 32 * FAR)], cfw_s)

    @pl.when(y >= 2)
    def _():
        gout_ref[...] = jnp.zeros_like(gout_ref)
        drain_send(cot_all.at[rows(0, 64 * FAR)], cfw_s)

    for which in range(3):
        @pl.when(y != which // 2)
        def _(which=which):
            cot_y_copy(which).wait_send()

    @pl.loop(1, 4)
    def _(j):
        k = (y + j) % 4
        y_copy(0, k, 0).wait_send()

        @pl.when(y == 0)
        def _():
            y_copy(1, k, 0).wait_send()

    drain_send(cot_all.at[rows(0, 64 * FAR)], cfar_s)
    drain_send(z_in.at[pl.ds(0, 7)], zin_s)
    drain_send(tok_all.at[rows(0, 992)], tok_s)


def finish_kernel(
    teacher_ref, tok_ref, dpre_ref, gout_ref, teacher_out, gin_out, gout_out, gin, sem
):
    t = lax.axis_index("tensor")
    w0 = pltpu.make_async_copy(gout_ref, gout_out, sem.at[0])
    w0.start()
    wt = pltpu.make_async_copy(teacher_ref, teacher_out, sem.at[3])
    wt.start()
    copies = [w0, wt]
    for h in range(2):
        part = pl.ds(h * 384, 384)

        @pl.when(t < 16)
        def _(h=h):
            gin[:, h * 384 : h * 384 + 384] = over_tokens(tok_ref[...], dpre_ref[h])

        @pl.when(t >= 16)
        def _(h=h):
            gin[:, h * 384 : h * 384 + 384] = jnp.zeros((384, 384), F32)

        w1 = pltpu.make_async_copy(gin.at[:, part], gin_out.at[:, part], sem.at[1 + h])
        w1.start()
        copies.append(w1)
    for w1 in copies:
        w1.wait()


def shards(tokens, in_weight, out_weight):
    vmem = pl.BlockSpec(memory_space=pltpu.VMEM)
    hbm = pl.BlockSpec(memory_space=pltpu.HBM)
    dma = pltpu.SemaphoreType.DMA
    one = dma(())
    block = pltpu.VMEM((8, 128, 384), BF16)
    flat = pltpu.VMEM((1024, 384), BF16)
    teacher, tok_all, dpre, grad_out = pl.pallas_call(
        kernel,
        out_shape=(
            jax.ShapeDtypeStruct((32, 384), BF16),
            jax.ShapeDtypeStruct((1024, 384), BF16),
            jax.ShapeDtypeStruct((2, 1024, 384), BF16),
            jax.ShapeDtypeStruct((768, 384), F32),
        ),
        in_specs=[hbm, hbm, hbm],
        out_specs=(vmem, vmem, vmem, vmem),
        scratch_shapes=[
            pltpu.VMEM((384, 768), BF16),
            pltpu.VMEM((768, 384), BF16),
            pltpu.VMEM((8, 16, 384), F32),
            pltpu.VMEM((2, 1024, 384), BF16),
            block,
            block,
            pltpu.VMEM((2, 4, 32, 384), BF16),
            pltpu.VMEM((5, 32, 384), BF16),
            pltpu.VMEM((3, 32, 384), BF16),
            pltpu.VMEM((2, 128, 384), BF16),
            pltpu.VMEM((8, 64, 384), BF16),
            flat,
        ]
        + [block, block, block, flat, flat] * 2
        + [
            dma((3,)),
            one, dma((8,)), dma((8,)),
            one, one,
            dma((2, 4)), dma((5,)),
            dma((3,)), dma((2, 4)),
            one, dma((8,)),
            one, dma((8,)), one, dma((8,)),
        ]
        + [one, dma((8,))] * 8,
        compiler_params=pltpu.CompilerParams(
            collective_id=0, has_side_effects=True, vmem_limit_bytes=32 * 1024 * 1024
        ),
        cost_estimate=pl.CostEstimate(
            flops=4 * 2 * 1024 * 384 * 768, bytes_accessed=4_000_000, transcendentals=100_000
        ),
    )(*[pltpu.with_memory_space_constraint(v, pltpu.HBM) for v in (tokens, in_weight, out_weight)])
    return pl.pallas_call(
        finish_kernel,
        out_shape=(
            jax.ShapeDtypeStruct((32, 384), BF16),
            jax.ShapeDtypeStruct((384, 768), F32),
            jax.ShapeDtypeStruct((768, 384), F32),
        ),
        in_specs=[vmem, vmem, vmem, vmem],
        out_specs=(hbm, hbm, hbm),
        scratch_shapes=[pltpu.VMEM((384, 768), F32), dma((4,))],
        compiler_params=pltpu.CompilerParams(vmem_limit_bytes=16 * 1024 * 1024),
        cost_estimate=pl.CostEstimate(
            flops=2 * 1024 * 384 * 768, bytes_accessed=4_000_000, transcendentals=0
        ),
    )(teacher, tok_all, dpre, grad_out)


def solution(mesh):
    in_specs = (P("tensor", "dp"), P("dp", "tensor"), P("tensor", "dp"))
    out_specs = (P("tensor", "dp"), P("dp", "tensor"), P("tensor", "dp"))
    return jax.shard_map(shards, mesh=mesh, in_specs=in_specs, out_specs=out_specs, check_vma=False)
```

```python
import jax
import jax.numpy as jnp
from jax import lax
from jax.experimental import pallas as pl
from jax.experimental.pallas import tpu as pltpu
from jax.sharding import PartitionSpec as P

inv_root_two = 0.7071067811865476
inv_root_tau = 0.3989422804014327
MESH = pl.DeviceIdType.MESH
BF16 = jnp.bfloat16
F32 = jnp.float32
FORWARD_LAGS = (1, 4, 7, 8)
BACKWARD_LAGS = (1, 6, 11, 12)
FAR = 3


def smooth_gate(values):
    return 0.5 * values * (1.0 + lax.erf(values * inv_root_two))


def gate_slope(values):
    return (
        0.5 * (1.0 + lax.erf(values * inv_root_two))
        + values * jnp.exp(-0.5 * values * values) * inv_root_tau
    )


def over_tokens(left, right):
    return lax.dot_general(
        left, right, (((0,), (0,)), ((), ())), preferred_element_type=F32
    )


def rows(start, size, step=None):
    return pl.ds(pl.multiple_of(start, step or size), size)


def kernel(
    tok_hbm, win_hbm, wout_hbm,
    teacher_ref, tok_all, dpre, gout_ref,
    win, wout, slope, hid, contrib, z_in, y_out, y_in,
    cots, cot_y, cot_far, cot_all,
    keep, give, sib_in, summed, rs_in,
    keep2, give2, sib_in2, summed2, rs_in2,
    wsem, tok_s, tok_r, far_r, zin_s, zin_r, yin_s, yin_r, cy_s, cy_r, ct_s, ct_r,
    cfar_s, cfar_r, cfw_s, cfw_r,
    sb_s, sb_r, rs_s, rs_r, ag_s, ag_r, rl_s, rl_r,
    sb2_s, sb2_r, rs2_s, rs2_r, ag2_s, ag2_r, rl2_s, rl2_r,
):
    d = lax.axis_index("dp")
    t = lax.axis_index("tensor")
    chip = d // 2
    core = d % 2
    sib = chip * 2 + 1 - core
    y = t // 8
    z = t % 8

    def remote(src, dst, s_sem, r_sem, dev):
        return pltpu.make_async_remote_copy(
            src_ref=src, dst_ref=dst, send_sem=s_sem, recv_sem=r_sem,
            device_id=dev, device_id_type=MESH,
        )

    def drain_send(ref, sem):
        remote(ref, ref, sem, sem, {"dp": sib}).wait_send()

    def drain_recv(ref, sem):
        remote(ref, ref, sem, sem, {"dp": sib}).wait_recv()

    def offset(i):
        n = (8 - i) % 8
        return ((n + 1) // 2) * (2 * (n % 2) - 1)

    def along_z(i):
        return (z + offset(i) + 8) % 8

    mine = tok_all.at[rows(y * 32, 32)]
    w0 = pltpu.make_async_copy(tok_hbm, mine, wsem.at[0])
    w1 = pltpu.make_async_copy(win_hbm, win, wsem.at[1])
    w2 = pltpu.make_async_copy(wout_hbm, wout, wsem.at[2])
    w0.start()
    w1.start()
    w2.start()

    barrier = pltpu.get_barrier_semaphore()

    @pl.loop(1, 8)
    def _(i):
        pl.semaphore_signal(
            barrier, inc=1, device_id={"tensor": y * 8 + (z + i) % 8}, device_id_type=MESH
        )
        pl.semaphore_signal(
            barrier, inc=1, device_id={"dp": ((chip + i) % 8) * 2 + core}, device_id_type=MESH
        )

    @pl.loop(1, 4)
    def _(i):
        pl.semaphore_signal(
            barrier, inc=1, device_id={"tensor": ((y + i) % 4) * 8 + z}, device_id_type=MESH
        )

    pl.semaphore_signal(barrier, inc=1, device_id={"dp": sib}, device_id_type=MESH)
    w0.wait()
    pl.semaphore_wait(barrier, 18)

    @pl.loop(1, FAR + 1)
    def _(i):
        remote(
            mine, tok_all.at[rows(i * 128 + y * 32, 32)], tok_s, tok_r.at[i],
            {"tensor": y * 8 + along_z(i)},
        ).start()

    @pl.loop(0, 3)
    def _(j):
        k = (y + 1 + (j + 1) % 3) % 4
        remote(mine, mine, tok_s, tok_r.at[0], {"tensor": k * 8 + z}).start()

    drain_recv(tok_all.at[rows(0, 96)], tok_r.at[0])

    @pl.loop(FAR + 1, 8)
    def _(i):
        remote(
            tok_all.at[rows(0, 128)], tok_all.at[rows(i * 128, 128)], tok_s, tok_r.at[i],
            {"tensor": y * 8 + along_z(i)},
        ).start()

    @pl.loop(1, FAR + 1)
    def _(i):
        part = tok_all.at[rows(i * 128 + y * 32, 32)]
        drain_recv(part, tok_r.at[i])

        @pl.loop(0, 3)
        def _(j):
            k = (y + 1 + (j + 1) % 3) % 4
            remote(part, part, tok_s, far_r.at[i], {"tensor": k * 8 + z}).start()

    w1.wait()
    w2.wait()

    def pipeline(
        lags, ready, block, finish, use, full_buf,
        keep, give, sib_in, summed, rs_in, sb_s, sb_r, rs_s, rs_r, ag_s, ag_r, rl_s, rl_r,
    ):
        def sib_copy(i):
            return remote(give.at[i], sib_in.at[i], sb_s, sb_r.at[i], {"dp": sib})

        def relay(i):
            place = full_buf.at[core, rows(i * 128, 128)]
            return remote(place, place, rl_s, rl_r.at[i], {"dp": sib})

        lag_sum, lag_hid, lag_all, lag_use = lags

        @pl.loop(0, 8 + lag_use)
        def _(s):
            @pl.when(s >= lag_use)
            def _():
                i = s - lag_use
                relay(i).wait_recv()
                use(i)

            @pl.when((s >= lag_all) & (s < lag_all + 8))
            def _():
                i = s - lag_all
                drain_recv(full_buf.at[core, rows(i * 128, 112, 128)], ag_r.at[i])
                relay(i).start()

            @pl.when((s >= lag_hid) & (s < lag_hid + 8))
            def _():
                i = s - lag_hid
                drain_recv(rs_in.at[rows(i * 128, 112, 128)], rs_r.at[i])
                total = jnp.zeros((16, 384), F32)
                for c in range(8):
                    total = total + rs_in[rows(i * 128 + c * 16, 16), :].astype(F32)
                own = rows(i * 128 + chip * 16, 16)
                full_buf[core, own, :] = finish(i, total)
                place = full_buf.at[core, own]

                @pl.loop(1, 8)
                def _(j):
                    c = (chip + j) % 8
                    remote(place, place, ag_s, ag_r.at[i], {"dp": c * 2 + core}).start()

            @pl.when((s >= lag_sum) & (s < lag_sum + 8))
            def _():
                i = s - lag_sum
                sib_copy(i).wait_recv()
                total = (keep[i].astype(F32) + sib_in[i].astype(F32)).astype(BF16)
                summed[rows(i * 128, 128), :] = total

                @pl.loop(1, 8)
                def _(j):
                    c = (chip + j) % 8
                    remote(
                        summed.at[rows(i * 128 + c * 16, 16)],
                        rs_in.at[rows(i * 128 + chip * 16, 16)],
                        rs_s, rs_r.at[i], {"dp": c * 2 + core},
                    ).start()

                own = rows(i * 128 + chip * 16, 16)
                rs_in[own, :] = summed[own, :]

            @pl.when(s < 8)
            def _():
                ready(s)
                term = block(s).astype(BF16)
                first, second = term[:, :384], term[:, 384:]
                keep[s] = jnp.where(core == 0, first, second)
                give[s] = jnp.where(core == 0, second, first)
                sib_copy(s).start()

        drain_send(give, sb_s)
        drain_send(summed.at[rows(0, 896)], rs_s)
        drain_send(full_buf.at[0, rows(0, 896)], ag_s)
        drain_send(full_buf.at[0], rl_s)

    def ready_of(all_ref, near_r, far_r, i):
        @pl.when(i > FAR)
        def _():
            drain_recv(all_ref.at[rows(i * 128, 128)], near_r.at[i])

        @pl.when((i > 0) & (i <= FAR))
        def _():
            drain_recv(all_ref.at[rows(i * 128, 96, 128)], far_r.at[i])

    def tok_ready(i):
        ready_of(tok_all, tok_r, far_r, i)

    def up(i):
        return jnp.dot(tok_all[rows(i * 128, 128), :], win[...], preferred_element_type=F32)

    def hidden_of(i, total):
        pre = total.astype(BF16).astype(F32)
        slope[i] = gate_slope(pre)
        return smooth_gate(pre).astype(BF16)

    def down(i):
        group = rows(i * 128, 128)
        out = jnp.dot(hid[0, group, :], wout[:384, :], preferred_element_type=F32)
        out = out + jnp.dot(hid[1, group, :], wout[384:, :], preferred_element_type=F32)

        @pl.when(i == 0)
        def _():
            z_in[z] = out.astype(BF16)

        @pl.when(i > 0)
        def _():
            contrib[i] = out.astype(BF16)
            dst = (z - offset(i) + 8) % 8
            remote(contrib.at[i], z_in.at[z], zin_s, zin_r, {"tensor": y * 8 + dst}).start()

    pipeline(
        FORWARD_LAGS, tok_ready, up, hidden_of, down, hid,
        keep, give, sib_in, summed, rs_in, sb_s, sb_r, rs_s, rs_r, ag_s, ag_r, rl_s, rl_r,
    )

    drain_recv(z_in.at[pl.ds(0, 7)], zin_r)

    def y_copy(which, k, slot):
        return remote(
            y_out.at[which, k], y_in.at[slot], yin_s.at[which, k], yin_r.at[slot],
            {"tensor": k * 8 + z},
        )

    slot = y + (y + 3) // 4

    @pl.loop(0, 4)
    def _(j):
        k = (y + 2 + j + j // 2 + j // 3 * 2) % 4
        part = rows(k * 32, 32)
        low = jnp.zeros((32, 384), F32)
        high = jnp.zeros((32, 384), F32)
        for s in range(4):
            low = low + z_in[s, part, :].astype(F32)
            high = high + z_in[s + 4, part, :].astype(F32)

        @pl.when(y == 0)
        def _():
            y_out[0, k] = low.astype(BF16)
            y_out[1, k] = high.astype(BF16)

        @pl.when(y > 0)
        def _():
            y_out[0, k] = (low + high).astype(BF16)

        @pl.when(k != y)
        def _():
            y_copy(0, k, slot).start()

            @pl.when(y == 0)
            def _():
                y_copy(1, k, 1).start()

        @pl.when(k == y)
        def _():
            y_in[slot] = y_out[0, k]

            @pl.when(y == 0)
            def _():
                y_in[1] = y_out[1, k]

    @pl.loop(0, 5)
    def _(s):
        @pl.when(s - (s + 4) // 5 != y)
        def _():
            y_copy(0, y, s).wait_recv()

    student_one = y_in[0].astype(F32)
    student_two = student_one + y_in[1].astype(F32)
    student_three = student_two + y_in[2].astype(F32)
    full = student_three + (y_in[3].astype(F32) + y_in[4].astype(F32))
    factor = 1.0 / 32.0
    diff_one = (student_one - full) * factor
    diff_two = (student_two - full) * factor
    diff_three = (student_three - full) * factor
    cots[0] = (diff_one + diff_two + diff_three).astype(BF16)
    cots[1] = (diff_two + diff_three).astype(BF16)
    cots[2] = diff_three.astype(BF16)

    def cot_y_copy(which):
        dst = which // 2
        return remote(
            cots.at[which], cot_y.at[which % 2, rows(y * 32, 32)], cy_s.at[which],
            cy_r.at[which % 2, y], {"tensor": dst * 8 + z},
        )

    for which in range(3):
        @pl.when(y != which // 2)
        def _(which=which):
            cot_y_copy(which).start()

        @pl.when(y == which // 2)
        def _(which=which):
            cot_y[which % 2, rows(y * 32, 32), :] = cots[which]

    @pl.loop(1, FAR + 1)
    def _(i):
        z_to = along_z(i)
        for row in range(2):
            kind = z_to // 4 if row == 0 else 2
            remote(
                cots.at[kind], cot_far.at[i, rows(row * 32, 32)], cfar_s, cfar_r.at[i],
                {"tensor": y * 8 + z_to},
            ).start()

    teacher_ref[...] = full.astype(BF16)

    @pl.when(y < 2)
    def _():
        @pl.loop(1, 4)
        def _(j):
            k = (y + j) % 4
            part = cot_y.at[0, rows(k * 32, 32)]
            drain_recv(part, cy_r.at[0, k])

            @pl.when(y == 0)
            def _():
                drain_recv(part, cy_r.at[1, k])

        @pl.loop(FAR + 1, 8)
        def _(i):
            kind = (1 - y) * (along_z(i) // 4)
            remote(
                cot_y.at[kind], cot_all.at[rows(i * 128, 128)], ct_s, ct_r.at[i],
                {"tensor": y * 8 + along_z(i)},
            ).start()

        cot_all[rows(0, 128), :] = cot_y[(1 - y) * (z // 4)]

    @pl.loop(1, FAR + 1)
    def _(i):
        drain_recv(cot_far.at[i], cfar_r.at[i])
        place = rows(i * 128 + y * 32, 32)
        for row in range(2):
            part = cot_far.at[i, rows(row * 32, 32)]

            @pl.when(y != row)
            def _(part=part, row=row):
                remote(
                    part, cot_all.at[place], cfw_s, cfw_r.at[i], {"tensor": row * 8 + z}
                ).start()

            @pl.when(y == row)
            def _(part=part):
                cot_all[place, :] = part[...]

    @pl.when(y < 2)
    def _():
        def cot_ready(i):
            ready_of(cot_all, ct_r, cfw_r, i)

        def back(i):
            return lax.dot_general(
                cot_all[rows(i * 128, 128), :], wout[...], (((1,), (1,)), ((), ())),
                preferred_element_type=F32,
            )

        def dpre_of(i, total):
            return (total * slope[i]).astype(BF16)

        def grads(i):
            @pl.when(i == 0)
            def _():
                for h in range(2):
                    gout_ref[h * 384 : h * 384 + 384, :] = over_tokens(hid[h], cot_all[...])

        pipeline(
            BACKWARD_LAGS, cot_ready, back, dpre_of, grads, dpre,
            keep2, give2, sib_in2, summed2, rs_in2,
            sb2_s, sb2_r, rs2_s, rs2_r, ag2_s, ag2_r, rl2_s, rl2_r,
        )
        drain_send(cot_all.at[rows(0, 128 * (7 - FAR))], ct_s)
        drain_send(cot_all.at[rows(0, 32 * FAR)], cfw_s)

    @pl.when(y >= 2)
    def _():
        gout_ref[...] = jnp.zeros_like(gout_ref)
        drain_send(cot_all.at[rows(0, 64 * FAR)], cfw_s)

    for which in range(3):
        @pl.when(y != which // 2)
        def _(which=which):
            cot_y_copy(which).wait_send()

    @pl.loop(1, 4)
    def _(j):
        k = (y + j) % 4
        y_copy(0, k, 0).wait_send()

        @pl.when(y == 0)
        def _():
            y_copy(1, k, 0).wait_send()

    drain_send(cot_all.at[rows(0, 64 * FAR)], cfar_s)
    drain_send(z_in.at[pl.ds(0, 7)], zin_s)
    drain_send(tok_all.at[rows(0, 992)], tok_s)


def finish_kernel(
    teacher_ref, tok_ref, dpre_ref, gout_ref, teacher_out, gin_out, gout_out, gin, sem
):
    t = lax.axis_index("tensor")
    w0 = pltpu.make_async_copy(gout_ref, gout_out, sem.at[0])
    w0.start()
    wt = pltpu.make_async_copy(teacher_ref, teacher_out, sem.at[3])
    wt.start()
    copies = [w0, wt]
    for h in range(2):
        part = pl.ds(h * 384, 384)

        @pl.when(t < 16)
        def _(h=h):
            gin[:, h * 384 : h * 384 + 384] = over_tokens(tok_ref[...], dpre_ref[h])

        @pl.when(t >= 16)
        def _(h=h):
            gin[:, h * 384 : h * 384 + 384] = jnp.zeros((384, 384), F32)

        w1 = pltpu.make_async_copy(gin.at[:, part], gin_out.at[:, part], sem.at[1 + h])
        w1.start()
        copies.append(w1)
    for w1 in copies:
        w1.wait()


def shards(tokens, in_weight, out_weight):
    vmem = pl.BlockSpec(memory_space=pltpu.VMEM)
    hbm = pl.BlockSpec(memory_space=pltpu.HBM)
    dma = pltpu.SemaphoreType.DMA
    one = dma(())
    block = pltpu.VMEM((8, 128, 384), BF16)
    flat = pltpu.VMEM((1024, 384), BF16)
    teacher, tok_all, dpre, grad_out = pl.pallas_call(
        kernel,
        out_shape=(
            jax.ShapeDtypeStruct((32, 384), BF16),
            jax.ShapeDtypeStruct((1024, 384), BF16),
            jax.ShapeDtypeStruct((2, 1024, 384), BF16),
            jax.ShapeDtypeStruct((768, 384), F32),
        ),
        in_specs=[hbm, hbm, hbm],
        out_specs=(vmem, vmem, vmem, vmem),
        scratch_shapes=[
            pltpu.VMEM((384, 768), BF16),
            pltpu.VMEM((768, 384), BF16),
            pltpu.VMEM((8, 16, 384), F32),
            pltpu.VMEM((2, 1024, 384), BF16),
            block,
            block,
            pltpu.VMEM((2, 4, 32, 384), BF16),
            pltpu.VMEM((5, 32, 384), BF16),
            pltpu.VMEM((3, 32, 384), BF16),
            pltpu.VMEM((2, 128, 384), BF16),
            pltpu.VMEM((8, 64, 384), BF16),
            flat,
        ]
        + [block, block, block, flat, flat] * 2
        + [
            dma((3,)),
            one, dma((8,)), dma((8,)),
            one, one,
            dma((2, 4)), dma((5,)),
            dma((3,)), dma((2, 4)),
            one, dma((8,)),
            one, dma((8,)), one, dma((8,)),
        ]
        + [one, dma((8,))] * 8,
        compiler_params=pltpu.CompilerParams(
            collective_id=0, has_side_effects=True, vmem_limit_bytes=32 * 1024 * 1024
        ),
        cost_estimate=pl.CostEstimate(
            flops=4 * 2 * 1024 * 384 * 768, bytes_accessed=4_000_000, transcendentals=100_000
        ),
    )(*[pltpu.with_memory_space_constraint(v, pltpu.HBM) for v in (tokens, in_weight, out_weight)])
    return pl.pallas_call(
        finish_kernel,
        out_shape=(
            jax.ShapeDtypeStruct((32, 384), BF16),
            jax.ShapeDtypeStruct((384, 768), F32),
            jax.ShapeDtypeStruct((768, 384), F32),
        ),
        in_specs=[vmem, vmem, vmem, vmem],
        out_specs=(hbm, hbm, hbm),
        scratch_shapes=[pltpu.VMEM((384, 768), F32), dma((4,))],
        compiler_params=pltpu.CompilerParams(vmem_limit_bytes=16 * 1024 * 1024),
        cost_estimate=pl.CostEstimate(
            flops=2 * 1024 * 384 * 768, bytes_accessed=4_000_000, transcendentals=0
        ),
    )(teacher, tok_all, dpre, grad_out)


def solution(mesh):
    in_specs = (P("tensor", "dp"), P("dp", "tensor"), P("tensor", "dp"))
    out_specs = (P("tensor", "dp"), P("dp", "tensor"), P("tensor", "dp"))
    return jax.shard_map(shards, mesh=mesh, in_specs=in_specs, out_specs=out_specs, check_vma=False)
```

```python
import jax
import jax.numpy as jnp
from jax import lax
from jax.experimental import pallas as pl
from jax.experimental.pallas import tpu as pltpu
from jax.sharding import PartitionSpec as P

inv_root_two = 0.7071067811865476
inv_root_tau = 0.3989422804014327
MESH = pl.DeviceIdType.MESH
BF16 = jnp.bfloat16
F32 = jnp.float32
FORWARD_LAGS = (1, 4, 7, 8)
BACKWARD_LAGS = (1, 6, 11, 12)
FAR = 3


def smooth_gate(values):
    return 0.5 * values * (1.0 + lax.erf(values * inv_root_two))


def gate_slope(values):
    return (
        0.5 * (1.0 + lax.erf(values * inv_root_two))
        + values * jnp.exp(-0.5 * values * values) * inv_root_tau
    )


def over_tokens(left, right):
    return lax.dot_general(
        left, right, (((0,), (0,)), ((), ())), preferred_element_type=F32
    )


def rows(start, size, step=None):
    return pl.ds(pl.multiple_of(start, step or size), size)


def kernel(
    tok_hbm, win_hbm, wout_hbm,
    teacher_ref, tok_all, dpre, gout_ref,
    win, wout, slope, hid, contrib, z_in, y_out, y_in,
    cots, cot_y, cot_far, cot_all,
    keep, give, sib_in, summed, rs_in,
    keep2, give2, sib_in2, summed2, rs_in2,
    wsem, tok_s, tok_r, far_r, zin_s, zin_r, yin_s, yin_r, cy_s, cy_r, ct_s, ct_r,
    cfar_s, cfar_r, cfw_s, cfw_r,
    sb_s, sb_r, rs_s, rs_r, ag_s, ag_r, rl_s, rl_r,
    sb2_s, sb2_r, rs2_s, rs2_r, ag2_s, ag2_r, rl2_s, rl2_r,
):
    d = lax.axis_index("dp")
    t = lax.axis_index("tensor")
    chip = d // 2
    core = d % 2
    sib = chip * 2 + 1 - core
    y = t // 8
    z = t % 8

    def remote(src, dst, s_sem, r_sem, dev):
        return pltpu.make_async_remote_copy(
            src_ref=src, dst_ref=dst, send_sem=s_sem, recv_sem=r_sem,
            device_id=dev, device_id_type=MESH,
        )

    def drain_send(ref, sem):
        remote(ref, ref, sem, sem, {"dp": sib}).wait_send()

    def drain_recv(ref, sem):
        remote(ref, ref, sem, sem, {"dp": sib}).wait_recv()

    def offset(i):
        n = (8 - i) % 8
        return ((n + 1) // 2) * (2 * (n % 2) - 1)

    def along_z(i):
        return (z + offset(i) + 8) % 8

    mine = tok_all.at[rows(y * 32, 32)]
    w0 = pltpu.make_async_copy(tok_hbm, mine, wsem.at[0])
    w1 = pltpu.make_async_copy(win_hbm, win, wsem.at[1])
    w2 = pltpu.make_async_copy(wout_hbm, wout, wsem.at[2])
    w0.start()
    w1.start()
    w2.start()

    barrier = pltpu.get_barrier_semaphore()

    @pl.loop(1, 8)
    def _(i):
        pl.semaphore_signal(
            barrier, inc=1, device_id={"tensor": y * 8 + (z + i) % 8}, device_id_type=MESH
        )
        pl.semaphore_signal(
            barrier, inc=1, device_id={"dp": ((chip + i) % 8) * 2 + core}, device_id_type=MESH
        )

    @pl.loop(1, 4)
    def _(i):
        pl.semaphore_signal(
            barrier, inc=1, device_id={"tensor": ((y + i) % 4) * 8 + z}, device_id_type=MESH
        )

    pl.semaphore_signal(barrier, inc=1, device_id={"dp": sib}, device_id_type=MESH)
    w0.wait()
    pl.semaphore_wait(barrier, 18)

    @pl.loop(0, 3)
    def _(j):
        k = (y + 1 + (j + 1) % 3) % 4
        remote(mine, mine, tok_s, tok_r.at[0], {"tensor": k * 8 + z}).start()

    @pl.loop(1, FAR + 1)
    def _(i):
        remote(
            mine, tok_all.at[rows(i * 128 + y * 32, 32)], tok_s, tok_r.at[i],
            {"tensor": y * 8 + along_z(i)},
        ).start()

    drain_recv(tok_all.at[rows(0, 96)], tok_r.at[0])

    @pl.loop(FAR + 1, 8)
    def _(i):
        remote(
            tok_all.at[rows(0, 128)], tok_all.at[rows(i * 128, 128)], tok_s, tok_r.at[i],
            {"tensor": y * 8 + along_z(i)},
        ).start()

    @pl.loop(1, FAR + 1)
    def _(i):
        part = tok_all.at[rows(i * 128 + y * 32, 32)]
        drain_recv(part, tok_r.at[i])

        @pl.loop(0, 3)
        def _(j):
            k = (y + 1 + (j + 1) % 3) % 4
            remote(part, part, tok_s, far_r.at[i], {"tensor": k * 8 + z}).start()

    w1.wait()
    w2.wait()

    def pipeline(
        lags, ready, block, finish, use, full_buf,
        keep, give, sib_in, summed, rs_in, sb_s, sb_r, rs_s, rs_r, ag_s, ag_r, rl_s, rl_r,
    ):
        def sib_copy(i):
            return remote(give.at[i], sib_in.at[i], sb_s, sb_r.at[i], {"dp": sib})

        def relay(i):
            place = full_buf.at[core, rows(i * 128, 128)]
            return remote(place, place, rl_s, rl_r.at[i], {"dp": sib})

        lag_sum, lag_hid, lag_all, lag_use = lags

        @pl.loop(0, 8 + lag_use)
        def _(s):
            @pl.when(s >= lag_use)
            def _():
                i = s - lag_use
                relay(i).wait_recv()
                use(i)

            @pl.when((s >= lag_all) & (s < lag_all + 8))
            def _():
                i = s - lag_all
                drain_recv(full_buf.at[core, rows(i * 128, 112, 128)], ag_r.at[i])
                relay(i).start()

            @pl.when((s >= lag_hid) & (s < lag_hid + 8))
            def _():
                i = s - lag_hid
                drain_recv(rs_in.at[rows(i * 128, 112, 128)], rs_r.at[i])
                total = jnp.zeros((16, 384), F32)
                for c in range(8):
                    total = total + rs_in[rows(i * 128 + c * 16, 16), :].astype(F32)
                own = rows(i * 128 + chip * 16, 16)
                full_buf[core, own, :] = finish(i, total)
                place = full_buf.at[core, own]

                @pl.loop(1, 8)
                def _(j):
                    c = (chip + j) % 8
                    remote(place, place, ag_s, ag_r.at[i], {"dp": c * 2 + core}).start()

            @pl.when((s >= lag_sum) & (s < lag_sum + 8))
            def _():
                i = s - lag_sum
                sib_copy(i).wait_recv()
                total = (keep[i].astype(F32) + sib_in[i].astype(F32)).astype(BF16)
                summed[rows(i * 128, 128), :] = total

                @pl.loop(1, 8)
                def _(j):
                    c = (chip + j) % 8
                    remote(
                        summed.at[rows(i * 128 + c * 16, 16)],
                        rs_in.at[rows(i * 128 + chip * 16, 16)],
                        rs_s, rs_r.at[i], {"dp": c * 2 + core},
                    ).start()

                own = rows(i * 128 + chip * 16, 16)
                rs_in[own, :] = summed[own, :]

            @pl.when(s < 8)
            def _():
                ready(s)
                term = block(s).astype(BF16)
                first, second = term[:, :384], term[:, 384:]
                keep[s] = jnp.where(core == 0, first, second)
                give[s] = jnp.where(core == 0, second, first)
                sib_copy(s).start()

        drain_send(give, sb_s)
        drain_send(summed.at[rows(0, 896)], rs_s)
        drain_send(full_buf.at[0, rows(0, 896)], ag_s)
        drain_send(full_buf.at[0], rl_s)

    def ready_of(all_ref, near_r, far_r, i):
        @pl.when(i > FAR)
        def _():
            drain_recv(all_ref.at[rows(i * 128, 128)], near_r.at[i])

        @pl.when((i > 0) & (i <= FAR))
        def _():
            drain_recv(all_ref.at[rows(i * 128, 96, 128)], far_r.at[i])

    def tok_ready(i):
        ready_of(tok_all, tok_r, far_r, i)

    def up(i):
        return jnp.dot(tok_all[rows(i * 128, 128), :], win[...], preferred_element_type=F32)

    def hidden_of(i, total):
        pre = total.astype(BF16).astype(F32)
        slope[i] = gate_slope(pre)
        return smooth_gate(pre).astype(BF16)

    def down(i):
        group = rows(i * 128, 128)
        out = jnp.dot(hid[0, group, :], wout[:384, :], preferred_element_type=F32)
        out = out + jnp.dot(hid[1, group, :], wout[384:, :], preferred_element_type=F32)

        @pl.when(i == 0)
        def _():
            z_in[z] = out.astype(BF16)

        @pl.when(i > 0)
        def _():
            contrib[i] = out.astype(BF16)
            dst = (z - offset(i) + 8) % 8
            remote(contrib.at[i], z_in.at[z], zin_s, zin_r, {"tensor": y * 8 + dst}).start()

    pipeline(
        FORWARD_LAGS, tok_ready, up, hidden_of, down, hid,
        keep, give, sib_in, summed, rs_in, sb_s, sb_r, rs_s, rs_r, ag_s, ag_r, rl_s, rl_r,
    )

    drain_recv(z_in.at[pl.ds(0, 7)], zin_r)

    def y_copy(which, k, slot):
        return remote(
            y_out.at[which, k], y_in.at[slot], yin_s.at[which, k], yin_r.at[slot],
            {"tensor": k * 8 + z},
        )

    slot = y + (y + 3) // 4

    @pl.loop(0, 4)
    def _(j):
        k = (y + 2 + j + j // 2 + j // 3 * 2) % 4
        part = rows(k * 32, 32)
        low = jnp.zeros((32, 384), F32)
        high = jnp.zeros((32, 384), F32)
        for s in range(4):
            low = low + z_in[s, part, :].astype(F32)
            high = high + z_in[s + 4, part, :].astype(F32)

        @pl.when(y == 0)
        def _():
            y_out[0, k] = low.astype(BF16)
            y_out[1, k] = high.astype(BF16)

        @pl.when(y > 0)
        def _():
            y_out[0, k] = (low + high).astype(BF16)

        @pl.when(k != y)
        def _():
            y_copy(0, k, slot).start()

            @pl.when(y == 0)
            def _():
                y_copy(1, k, 1).start()

        @pl.when(k == y)
        def _():
            y_in[slot] = y_out[0, k]

            @pl.when(y == 0)
            def _():
                y_in[1] = y_out[1, k]

    @pl.loop(0, 5)
    def _(s):
        @pl.when(s - (s + 4) // 5 != y)
        def _():
            y_copy(0, y, s).wait_recv()

    student_one = y_in[0].astype(F32)
    student_two = student_one + y_in[1].astype(F32)
    student_three = student_two + y_in[2].astype(F32)
    full = student_three + (y_in[3].astype(F32) + y_in[4].astype(F32))
    factor = 1.0 / 32.0
    diff_one = (student_one - full) * factor
    diff_two = (student_two - full) * factor
    diff_three = (student_three - full) * factor
    cots[0] = (diff_one + diff_two + diff_three).astype(BF16)
    cots[1] = (diff_two + diff_three).astype(BF16)
    cots[2] = diff_three.astype(BF16)

    def cot_y_copy(which):
        dst = which // 2
        return remote(
            cots.at[which], cot_y.at[which % 2, rows(y * 32, 32)], cy_s.at[which],
            cy_r.at[which % 2, y], {"tensor": dst * 8 + z},
        )

    for which in range(3):
        @pl.when(y != which // 2)
        def _(which=which):
            cot_y_copy(which).start()

        @pl.when(y == which // 2)
        def _(which=which):
            cot_y[which % 2, rows(y * 32, 32), :] = cots[which]

    @pl.loop(1, FAR + 1)
    def _(i):
        z_to = along_z(i)
        for row in range(2):
            kind = z_to // 4 if row == 0 else 2
            remote(
                cots.at[kind], cot_far.at[i, rows(row * 32, 32)], cfar_s, cfar_r.at[i],
                {"tensor": y * 8 + z_to},
            ).start()

    teacher_ref[...] = full.astype(BF16)

    @pl.when(y < 2)
    def _():
        @pl.loop(1, 4)
        def _(j):
            k = (y + j) % 4
            part = cot_y.at[0, rows(k * 32, 32)]
            drain_recv(part, cy_r.at[0, k])

            @pl.when(y == 0)
            def _():
                drain_recv(part, cy_r.at[1, k])

        @pl.loop(FAR + 1, 8)
        def _(i):
            kind = (1 - y) * (along_z(i) // 4)
            remote(
                cot_y.at[kind], cot_all.at[rows(i * 128, 128)], ct_s, ct_r.at[i],
                {"tensor": y * 8 + along_z(i)},
            ).start()

        cot_all[rows(0, 128), :] = cot_y[(1 - y) * (z // 4)]

    @pl.loop(1, FAR + 1)
    def _(i):
        drain_recv(cot_far.at[i], cfar_r.at[i])
        place = rows(i * 128 + y * 32, 32)
        for row in range(2):
            part = cot_far.at[i, rows(row * 32, 32)]

            @pl.when(y != row)
            def _(part=part, row=row):
                remote(
                    part, cot_all.at[place], cfw_s, cfw_r.at[i], {"tensor": row * 8 + z}
                ).start()

            @pl.when(y == row)
            def _(part=part):
                cot_all[place, :] = part[...]

    @pl.when(y < 2)
    def _():
        def cot_ready(i):
            ready_of(cot_all, ct_r, cfw_r, i)

        def back(i):
            return lax.dot_general(
                cot_all[rows(i * 128, 128), :], wout[...], (((1,), (1,)), ((), ())),
                preferred_element_type=F32,
            )

        def dpre_of(i, total):
            return (total * slope[i]).astype(BF16)

        def grads(i):
            @pl.when(i == 0)
            def _():
                for h in range(2):
                    gout_ref[h * 384 : h * 384 + 384, :] = over_tokens(hid[h], cot_all[...])

        pipeline(
            BACKWARD_LAGS, cot_ready, back, dpre_of, grads, dpre,
            keep2, give2, sib_in2, summed2, rs_in2,
            sb2_s, sb2_r, rs2_s, rs2_r, ag2_s, ag2_r, rl2_s, rl2_r,
        )
        drain_send(cot_all.at[rows(0, 128 * (7 - FAR))], ct_s)
        drain_send(cot_all.at[rows(0, 32 * FAR)], cfw_s)

    @pl.when(y >= 2)
    def _():
        gout_ref[...] = jnp.zeros_like(gout_ref)
        drain_send(cot_all.at[rows(0, 64 * FAR)], cfw_s)

    for which in range(3):
        @pl.when(y != which // 2)
        def _(which=which):
            cot_y_copy(which).wait_send()

    @pl.loop(1, 4)
    def _(j):
        k = (y + j) % 4
        y_copy(0, k, 0).wait_send()

        @pl.when(y == 0)
        def _():
            y_copy(1, k, 0).wait_send()

    drain_send(cot_all.at[rows(0, 64 * FAR)], cfar_s)
    drain_send(z_in.at[pl.ds(0, 7)], zin_s)
    drain_send(tok_all.at[rows(0, 992)], tok_s)


def finish_kernel(
    teacher_ref, tok_ref, dpre_ref, gout_ref, teacher_out, gin_out, gout_out, gin, sem
):
    t = lax.axis_index("tensor")
    w0 = pltpu.make_async_copy(gout_ref, gout_out, sem.at[0])
    w0.start()
    wt = pltpu.make_async_copy(teacher_ref, teacher_out, sem.at[3])
    wt.start()
    copies = [w0, wt]
    for h in range(2):
        part = pl.ds(h * 384, 384)

        @pl.when(t < 16)
        def _(h=h):
            gin[:, h * 384 : h * 384 + 384] = over_tokens(tok_ref[...], dpre_ref[h])

        @pl.when(t >= 16)
        def _(h=h):
            gin[:, h * 384 : h * 384 + 384] = jnp.zeros((384, 384), F32)

        w1 = pltpu.make_async_copy(gin.at[:, part], gin_out.at[:, part], sem.at[1 + h])
        w1.start()
        copies.append(w1)
    for w1 in copies:
        w1.wait()


def shards(tokens, in_weight, out_weight):
    vmem = pl.BlockSpec(memory_space=pltpu.VMEM)
    hbm = pl.BlockSpec(memory_space=pltpu.HBM)
    dma = pltpu.SemaphoreType.DMA
    one = dma(())
    block = pltpu.VMEM((8, 128, 384), BF16)
    flat = pltpu.VMEM((1024, 384), BF16)
    teacher, tok_all, dpre, grad_out = pl.pallas_call(
        kernel,
        out_shape=(
            jax.ShapeDtypeStruct((32, 384), BF16),
            jax.ShapeDtypeStruct((1024, 384), BF16),
            jax.ShapeDtypeStruct((2, 1024, 384), BF16),
            jax.ShapeDtypeStruct((768, 384), F32),
        ),
        in_specs=[hbm, hbm, hbm],
        out_specs=(vmem, vmem, vmem, vmem),
        scratch_shapes=[
            pltpu.VMEM((384, 768), BF16),
            pltpu.VMEM((768, 384), BF16),
            pltpu.VMEM((8, 16, 384), F32),
            pltpu.VMEM((2, 1024, 384), BF16),
            block,
            block,
            pltpu.VMEM((2, 4, 32, 384), BF16),
            pltpu.VMEM((5, 32, 384), BF16),
            pltpu.VMEM((3, 32, 384), BF16),
            pltpu.VMEM((2, 128, 384), BF16),
            pltpu.VMEM((8, 64, 384), BF16),
            flat,
        ]
        + [block, block, block, flat, flat] * 2
        + [
            dma((3,)),
            one, dma((8,)), dma((8,)),
            one, one,
            dma((2, 4)), dma((5,)),
            dma((3,)), dma((2, 4)),
            one, dma((8,)),
            one, dma((8,)), one, dma((8,)),
        ]
        + [one, dma((8,))] * 8,
        compiler_params=pltpu.CompilerParams(
            collective_id=0, has_side_effects=True, vmem_limit_bytes=32 * 1024 * 1024
        ),
        cost_estimate=pl.CostEstimate(
            flops=4 * 2 * 1024 * 384 * 768, bytes_accessed=4_000_000, transcendentals=100_000
        ),
    )(*[pltpu.with_memory_space_constraint(v, pltpu.HBM) for v in (tokens, in_weight, out_weight)])
    return pl.pallas_call(
        finish_kernel,
        out_shape=(
            jax.ShapeDtypeStruct((32, 384), BF16),
            jax.ShapeDtypeStruct((384, 768), F32),
            jax.ShapeDtypeStruct((768, 384), F32),
        ),
        in_specs=[vmem, vmem, vmem, vmem],
        out_specs=(hbm, hbm, hbm),
        scratch_shapes=[pltpu.VMEM((384, 768), F32), dma((4,))],
        compiler_params=pltpu.CompilerParams(vmem_limit_bytes=16 * 1024 * 1024),
        cost_estimate=pl.CostEstimate(
            flops=2 * 1024 * 384 * 768, bytes_accessed=4_000_000, transcendentals=0
        ),
    )(teacher, tok_all, dpre, grad_out)


def solution(mesh):
    in_specs = (P("tensor", "dp"), P("dp", "tensor"), P("tensor", "dp"))
    out_specs = (P("tensor", "dp"), P("dp", "tensor"), P("tensor", "dp"))
    return jax.shard_map(shards, mesh=mesh, in_specs=in_specs, out_specs=out_specs, check_vma=False)
```
